32 devices in a mesh: hot: 8 (over y, x, core), load: 4 (over z).
Axes of the slice: x: 2, y: 2, z: 4, core: 2. Of those that a mesh axis runs over, the one named last changes fastest.
Arguments:
- response: bfloat16 [2048, 2048, 128], P('hot', 'load'), may hold values from -1 to 1, as said below
- forces: bfloat16 [2048, 1408], P('load'), may hold values from -6 to 6
- measured: float32 [2048, 384], P('hot'), may hold values from -6 to 6
Outputs:
- updated_forces: float32 [2048, 1408], P('load')
- updated_residual: float32 [2048, 384], P('hot')
The draws below stay inside these ranges and needn't reach their ends.
Inputs may be any that keep to these rules, and one draw needn't show every extreme that they name: impulse-response coefficients.
All inputs are finite; a program needn't handle non-finite values.
Results may differ from the reference program's by a relative error of at most 0.0041.
Values sent between devices are 32-bit elements; how exact they have to be, the bound alone decides.
A program may use at most 448 MiB of HBM per device.

```python
import jax
import jax.numpy as jnp
from jax import lax

HOTSPOTS = 2048
LOADS = 2048
TAPS = 128
SEG = 48
CASES = 8
HIST = 128
STEPS = 176


def draw_response(key, part):
    shape = (HOTSPOTS, LOADS, TAPS)
    first_key = jax.random.fold_in(key, 0)
    hot_pos = jnp.arange(HOTSPOTS, dtype=jnp.float32)[:, None, None] / (HOTSPOTS - 1)
    load_pos = jnp.arange(LOADS, dtype=jnp.float32)[None, :, None] / (LOADS - 1)
    rising = jnp.exp(jnp.log(3.0) * (hot_pos + load_pos))
    base = jax.random.truncated_normal(first_key, -6.0, 6.0, shape, jnp.float32)
    values = base * rising
    values = values / (2.0 * jnp.sqrt(jnp.float32(LOADS * TAPS)))
    return values.astype(jnp.bfloat16)


def levels(own_key, dims, pieces, least, top_value):
    def one(position, shards_of):
        heights = jax.random.uniform(jax.random.fold_in(jax.random.fold_in(own_key, 6), position), (shards_of,), jnp.float32, least / len(pieces), top_value / len(pieces))
        return jnp.repeat(jnp.exp(heights), dims[position] // shards_of).reshape((-1,) + (1,) * (len(dims) - position - 1))

    level = one(*pieces[0])
    for cut in pieces[1:]:
        level = level * one(*cut)
    return level


def normal_values(own_key, shape, deviation, most, shards=(), held_as=jnp.bfloat16):
    level = levels(own_key, shape, shards, -0.22, 0.18) if shards else 1.0
    result = jax.random.normal(own_key, shape, jnp.float32) * deviation * level
    return jnp.minimum(jnp.maximum(result, -most), most).astype(held_as)


def setup_inputs(seed: int = 0) -> dict:
    key_of = jax.random.split(jax.random.key(seed), 4)
    response = draw_response(jax.random.fold_in(key_of[3], 71), 0)
    forces = normal_values(key_of[1], (LOADS, STEPS * CASES), 1.0, 6.0, ((0, 4),))
    measured = normal_values(key_of[2], (HOTSPOTS, SEG * CASES), 1.0, 6.0, ((0, 8),), jnp.float32)
    return dict(response=response, forces=forces, measured=measured)


def strain_product(response, signal):
    seg_cols = SEG * CASES
    running = jnp.zeros((response.shape[0], seg_cols), jnp.float32)
    tap_span = min(16, TAPS)
    for first_tap in range(0, TAPS, tap_span):
        tap_block = response[:, :, first_tap:first_tap + tap_span].astype(jnp.float32)
        window = jnp.stack([signal[:, (HIST - tap_index) * CASES:(HIST - tap_index) * CASES + seg_cols]
                            for tap_index in range(first_tap, first_tap + tap_span)], axis=1).astype(jnp.float32)
        running = running + jnp.einsum('hlk,lkm->hm', tap_block, window, precision=lax.Precision.HIGHEST)
    return running


def load_product(response, strains):
    col_count = STEPS * CASES
    padded = jnp.pad(strains.astype(jnp.float32), ((0, 0), (HIST * CASES, TAPS * CASES)))
    running = jnp.zeros((response.shape[1], col_count), jnp.float32)
    tap_span = min(16, TAPS)
    for first_tap in range(0, TAPS, tap_span):
        tap_block = response[:, :, first_tap:first_tap + tap_span].astype(jnp.float32)
        window = jnp.stack([padded[:, tap_index * CASES:tap_index * CASES + col_count]
                            for tap_index in range(first_tap, first_tap + tap_span)], axis=1)
        running = running + jnp.einsum('hlk,hkm->lm', tap_block, window, precision=lax.Precision.HIGHEST)
    return running


def reference(response, forces, measured):
    strains = strain_product(response, forces)
    residual = measured - strains
    residual_b = residual.astype(jnp.bfloat16)
    gradient = load_product(response, residual_b)
    gradient_b = gradient.astype(jnp.bfloat16)
    image_sum = strain_product(response, gradient_b)
    step_size = jnp.sum(gradient * gradient) / jnp.sum(image_sum * image_sum)
    return forces.astype(jnp.float32) + step_size * gradient, residual - step_size * image_sum
```

```python
import functools

import jax
import jax.numpy as jnp
from jax import lax
from jax.experimental import pallas as pl
from jax.experimental.pallas import tpu as pltpu
from jax.sharding import PartitionSpec as P

TAPS = 128
SEG = 48
CASES = 8
HIST = 128
STEPS = 176
COLS = STEPS * CASES
SEG_COLS = SEG * CASES
MIB = 1 << 20

STEP_TAPS = 8
GROUP = 4
WINDOW = -(-(SEG_COLS + (GROUP - 1) * CASES) // 16) * 16


def tap_major_kernel(hots, in_ref, out_ref, held):
    lanes = held.shape[2]
    for part in range(held.shape[0]):
        loads = slice(part * lanes, (part + 1) * lanes)
        for h in range(hots):
            held[part, pl.ds(h, TAPS, stride=hots), :] = in_ref[h, loads, :].T.astype(jnp.float32)
        out_ref[:, :, loads] = held[part].astype(jnp.bfloat16).reshape(TAPS, hots, lanes)


def tap_major(response):
    hots, loads, taps = response.shape
    block = 16
    return pl.pallas_call(
        functools.partial(tap_major_kernel, block),
        grid=(hots // block,),
        in_specs=[pl.BlockSpec((block, loads, taps), lambda i: (i, 0, 0))],
        out_specs=pl.BlockSpec((taps, block, loads), lambda i: (0, i, 0)),
        out_shape=jax.ShapeDtypeStruct((taps, hots, loads), response.dtype),
        scratch_shapes=[pltpu.VMEM((loads // 128, taps * block, 128), jnp.float32)],
        compiler_params=pltpu.CompilerParams(vmem_limit_bytes=40 * MIB),
        cost_estimate=pl.CostEstimate(
            flops=0, bytes_accessed=4 * response.size, transcendentals=0
        ),
        name="tap_major",
    )(response)


def strain_kernel(even_ref, odd_ref, tile_ref, out_ref):
    step = pl.program_id(0)

    @pl.when(step == 0)
    def _():
        out_ref[...] = jnp.zeros_like(out_ref)

    total = out_ref[...]
    for i in range(STEP_TAPS):
        parity = (HIST - i) % 2
        signal_ref = odd_ref if parity else even_ref
        first = (HIST - i - parity) * CASES - step * (STEP_TAPS * CASES)
        rows = pl.ds(pl.multiple_of(first, 16), SEG_COLS)
        total += lax.dot_general(
            signal_ref[rows, :],
            tile_ref[i],
            (((1,), (1,)), ((), ())),
            preferred_element_type=jnp.float32,
        )
    out_ref[...] = total


def strain_product(tiles, signal):
    taps, hots, loads = tiles.shape
    odd = jnp.concatenate([signal[CASES:], signal[:CASES]])
    whole = pl.BlockSpec((COLS, loads), lambda i: (0, 0))
    return pl.pallas_call(
        strain_kernel,
        grid=(taps // STEP_TAPS,),
        in_specs=[whole, whole, pl.BlockSpec((STEP_TAPS, hots, loads), lambda i: (i, 0, 0))],
        out_specs=pl.BlockSpec((SEG_COLS, hots), lambda i: (0, 0)),
        out_shape=jax.ShapeDtypeStruct((SEG_COLS, hots), jnp.float32),
        compiler_params=pltpu.CompilerParams(vmem_limit_bytes=40 * MIB),
        cost_estimate=pl.CostEstimate(
            flops=2 * SEG_COLS * tiles.size, bytes_accessed=2 * tiles.size, transcendentals=0
        ),
        name="strain_product",
    )(signal, odd, tiles)


def gradient_kernel(hots, strains_ref, tile_ref, out_ref, held):
    step = pl.program_id(0)

    @pl.when(step == 0)
    def _():
        held[...] = jnp.zeros_like(held)

    for i in range(0, STEP_TAPS, GROUP):
        first = (HIST - i - (GROUP - 1)) * CASES - step * (STEP_TAPS * CASES)
        rows = pl.ds(pl.multiple_of(first, CASES), WINDOW)
        tile = tile_ref[i : i + GROUP].reshape(GROUP * hots, tile_ref.shape[2])
        held[rows, :] += jnp.dot(strains_ref[...], tile, preferred_element_type=jnp.float32)

    @pl.when(step == TAPS // STEP_TAPS - 1)
    def _():
        out_ref[...] = held[:COLS, :]


def load_product(tiles, strains):
    taps, hots, loads = tiles.shape
    stacked = jnp.concatenate(
        [
            jnp.pad(
                strains,
                (((GROUP - 1 - i) * CASES, WINDOW - SEG_COLS - (GROUP - 1 - i) * CASES), (0, 0)),
            )
            for i in range(GROUP)
        ],
        axis=1,
    )
    return pl.pallas_call(
        functools.partial(gradient_kernel, hots),
        grid=(taps // STEP_TAPS,),
        in_specs=[
            pl.BlockSpec((WINDOW, GROUP * hots), lambda i: (0, 0)),
            pl.BlockSpec((STEP_TAPS, hots, loads), lambda i: (i, 0, 0)),
        ],
        out_specs=pl.BlockSpec((COLS, loads), lambda i: (0, 0)),
        out_shape=jax.ShapeDtypeStruct((COLS, loads), jnp.float32),
        scratch_shapes=[pltpu.VMEM((COLS + 16, loads), jnp.float32)],
        compiler_params=pltpu.CompilerParams(vmem_limit_bytes=40 * MIB),
        cost_estimate=pl.CostEstimate(
            flops=2 * WINDOW * tiles.size, bytes_accessed=2 * tiles.size, transcendentals=0
        ),
        name="load_product",
    )(stacked, tiles)


def body(response, forces, measured):
    tiles = tap_major(response)
    strains = lax.psum(strain_product(tiles, forces.T), "load")
    residual = measured.T - strains
    gradient = lax.psum(load_product(tiles, residual.astype(jnp.bfloat16)), "hot")
    grad_total = lax.psum(jnp.sum(gradient * gradient), "load")
    image = lax.psum(strain_product(tiles, gradient.astype(jnp.bfloat16)), "load")
    image_total = lax.psum(jnp.sum(image * image), "hot")
    step_size = grad_total / image_total
    updated_forces = forces.astype(jnp.float32) + step_size * gradient.T
    return updated_forces, (residual - step_size * image).T


def solution(mesh):
    placed = (P("hot", "load", None), P("load", None), P("hot", None))
    return jax.shard_map(
        body,
        mesh=mesh,
        in_specs=placed,
        out_specs=(P("load", None), P("hot", None)),
        check_vma=False,
    )
```

```python
import functools

import jax
import jax.numpy as jnp
from jax import lax
from jax.experimental import pallas as pl
from jax.experimental.pallas import tpu as pltpu
from jax.sharding import PartitionSpec as P

TAPS = 128
SEG = 48
CASES = 8
HIST = 128
STEPS = 176
COLS = STEPS * CASES
SEG_COLS = SEG * CASES
MIB = 1 << 20

GROUP = 4
STREAMS = 4
STEP_TAPS = GROUP * STREAMS
WINDOW = -(-(SEG_COLS + (GROUP - 1) * CASES) // 16) * 16


def tap_major_kernel(hots, in_ref, out_ref, held):
    lanes = held.shape[2]
    for part in range(held.shape[0]):
        loads = slice(part * lanes, (part + 1) * lanes)
        for h in range(hots):
            held[part, pl.ds(h, TAPS, stride=hots), :] = in_ref[h, loads, :].T.astype(jnp.float32)
        out_ref[:, :, loads] = held[part].astype(jnp.bfloat16).reshape(TAPS, hots, lanes)


def tap_major(response):
    hots, loads, taps = response.shape
    block = 16
    return pl.pallas_call(
        functools.partial(tap_major_kernel, block),
        grid=(hots // block,),
        in_specs=[pl.BlockSpec((block, loads, taps), lambda i: (i, 0, 0))],
        out_specs=pl.BlockSpec((taps, block, loads), lambda i: (0, i, 0)),
        out_shape=jax.ShapeDtypeStruct((taps, hots, loads), response.dtype),
        scratch_shapes=[pltpu.VMEM((loads // 128, taps * block, 128), jnp.float32)],
        compiler_params=pltpu.CompilerParams(vmem_limit_bytes=40 * MIB),
        cost_estimate=pl.CostEstimate(
            flops=0, bytes_accessed=4 * response.size, transcendentals=0
        ),
        name="tap_major",
    )(response)


def tile_specs(hots, loads):
    return [
        pl.BlockSpec((GROUP, hots, loads), lambda i, part=part: (i * STREAMS + part, 0, 0))
        for part in range(STREAMS)
    ]


def strain_kernel(even_ref, odd_ref, *refs):
    *tile_refs, out_ref = refs
    step = pl.program_id(0)

    @pl.when(step == 0)
    def _():
        out_ref[...] = jnp.zeros_like(out_ref)

    total = out_ref[...]
    for i in range(STEP_TAPS):
        parity = (HIST - i) % 2
        signal_ref = odd_ref if parity else even_ref
        first = (HIST - i - parity) * CASES - step * (STEP_TAPS * CASES)
        rows = pl.ds(pl.multiple_of(first, 16), SEG_COLS)
        total += lax.dot_general(
            signal_ref[rows, :],
            tile_refs[i // GROUP][i % GROUP],
            (((1,), (1,)), ((), ())),
            preferred_element_type=jnp.float32,
        )
    out_ref[...] = total


def strain_product(tiles, signal):
    taps, hots, loads = tiles.shape
    odd = jnp.concatenate([signal[CASES:], signal[:CASES]])
    whole = pl.BlockSpec((COLS, loads), lambda i: (0, 0))
    return pl.pallas_call(
        strain_kernel,
        grid=(taps // STEP_TAPS,),
        in_specs=[whole, whole, *tile_specs(hots, loads)],
        out_specs=pl.BlockSpec((SEG_COLS, hots), lambda i: (0, 0)),
        out_shape=jax.ShapeDtypeStruct((SEG_COLS, hots), jnp.float32),
        compiler_params=pltpu.CompilerParams(vmem_limit_bytes=40 * MIB),
        cost_estimate=pl.CostEstimate(
            flops=2 * SEG_COLS * tiles.size, bytes_accessed=2 * tiles.size, transcendentals=0
        ),
        name="strain_product",
    )(signal, odd, *[tiles] * STREAMS)


def gradient_kernel(hots, strains_ref, *refs):
    *tile_refs, out_ref, held = refs
    step = pl.program_id(0)

    @pl.when(step == 0)
    def _():
        held[...] = jnp.zeros_like(held)

    for i in range(0, STEP_TAPS, GROUP):
        first = (HIST - i - (GROUP - 1)) * CASES - step * (STEP_TAPS * CASES)
        rows = pl.ds(pl.multiple_of(first, CASES), WINDOW)
        tile_ref = tile_refs[i // GROUP]
        tile = tile_ref[...].reshape(GROUP * hots, tile_ref.shape[2])
        held[rows, :] += jnp.dot(strains_ref[...], tile, preferred_element_type=jnp.float32)

    @pl.when(step == TAPS // STEP_TAPS - 1)
    def _():
        out_ref[...] = held[: out_ref.shape[0], :]


def load_product(tiles, strains, parts):
    taps, hots, loads = tiles.shape
    rows = -(-COLS // (8 * parts)) * 8 * parts
    stacked = jnp.concatenate(
        [
            jnp.pad(
                strains,
                (((GROUP - 1 - i) * CASES, WINDOW - SEG_COLS - (GROUP - 1 - i) * CASES), (0, 0)),
            )
            for i in range(GROUP)
        ],
        axis=1,
    )
    return pl.pallas_call(
        functools.partial(gradient_kernel, hots),
        grid=(taps // STEP_TAPS,),
        in_specs=[
            pl.BlockSpec((WINDOW, GROUP * hots), lambda i: (0, 0)),
            *tile_specs(hots, loads),
        ],
        out_specs=pl.BlockSpec((rows, loads), lambda i: (0, 0)),
        out_shape=jax.ShapeDtypeStruct((rows, loads), jnp.float32),
        scratch_shapes=[pltpu.VMEM((max(rows, COLS + 16), loads), jnp.float32)],
        compiler_params=pltpu.CompilerParams(vmem_limit_bytes=40 * MIB),
        cost_estimate=pl.CostEstimate(
            flops=2 * WINDOW * tiles.size, bytes_accessed=2 * tiles.size, transcendentals=0
        ),
        name="load_product",
    )(stacked, *[tiles] * STREAMS)


def greet(peers):
    barrier = pltpu.get_barrier_semaphore()
    for peer in peers:
        pl.semaphore_signal(
            barrier, inc=1, device_id=peer, device_id_type=pl.DeviceIdType.MESH
        )
    pl.semaphore_wait(barrier, len(peers))


def send(source, target, send_sem, recv_sem, peer):
    copy = pltpu.make_async_remote_copy(
        src_ref=source,
        dst_ref=target,
        send_sem=send_sem,
        recv_sem=recv_sem,
        device_id=peer,
        device_id_type=pl.DeviceIdType.MESH,
    )
    copy.start()
    return copy


def other(axis, count, step):
    return {axis: lax.rem(lax.axis_index(axis) + step, count)}


def add_over_load(count, in_ref, out_ref, parts, sems):
    me = lax.axis_index("load")
    chunk = in_ref.shape[0] // count

    def rows(index):
        return pl.ds(pl.multiple_of(index * chunk, 8), chunk)

    copies = []
    for step in range(1, count):
        peer = other("load", count, step)
        copies.append(
            send(
                in_ref.at[rows(peer["load"])],
                parts.at[step - 1],
                sems.at[0, step - 1],
                sems.at[1, step - 1],
                peer,
            )
        )
    total = in_ref[rows(me), :]
    for step, copy in enumerate(copies):
        copy.wait()
        total += parts[step]
    out_ref[rows(me), :] = total
    copies = []
    for step in range(1, count):
        mine = out_ref.at[rows(me)]
        peer = other("load", count, step)
        copies.append(send(mine, mine, sems.at[2, step - 1], sems.at[3, step - 1], peer))
    for copy in copies:
        copy.wait()


def load_sum_kernel(count, in_ref, out_ref, parts, sems):
    greet([other("load", count, step) for step in range(1, count)])
    add_over_load(count, in_ref, out_ref, parts, sems)


def load_sum(terms, count):
    rows, cols = terms.shape
    return pl.pallas_call(
        functools.partial(load_sum_kernel, count),
        in_specs=[pl.BlockSpec(memory_space=pltpu.VMEM)],
        out_specs=pl.BlockSpec(memory_space=pltpu.VMEM),
        out_shape=jax.ShapeDtypeStruct(terms.shape, terms.dtype),
        scratch_shapes=[
            pltpu.VMEM((count - 1, rows // count, cols), jnp.float32),
            pltpu.SemaphoreType.DMA((4, count - 1)),
        ],
        compiler_params=pltpu.CompilerParams(
            collective_id=0, has_side_effects=True, vmem_limit_bytes=40 * MIB
        ),
        name="load_sum",
    )(terms)


def image_sum_kernel(
    loads, hots, in_ref, norm_ref, out_ref, step_ref, parts, load_norms, hot_norms, sems, load_sems, hot_sems
):
    load, hot = lax.axis_index("load"), lax.axis_index("hot")
    load_peers = [other("load", loads, step) for step in range(1, loads)]
    hot_peers = [other("hot", hots, step) for step in range(1, hots)]
    greet(load_peers + hot_peers)

    load_norms[load] = norm_ref[...]
    copies = []
    for i, peer in enumerate(load_peers):
        mine = load_norms.at[load]
        copies.append(send(mine, mine, load_sems.at[0, i], load_sems.at[1, i], peer))
    add_over_load(loads, in_ref, out_ref, parts, sems)
    image = out_ref[...]
    hot_norms[hot] = jnp.full(hot_norms.shape[1:], jnp.sum(image * image))
    for i, peer in enumerate(hot_peers):
        mine = hot_norms.at[hot]
        copies.append(send(mine, mine, hot_sems.at[0, i], hot_sems.at[1, i], peer))
    for copy in copies:
        copy.wait()
    step_ref[...] = jnp.sum(load_norms[...], axis=0) / jnp.sum(hot_norms[...], axis=0)


def image_sum(terms, norm, loads, hots):
    rows, cols = terms.shape
    tile = (8, 128)
    vmem = pl.BlockSpec(memory_space=pltpu.VMEM)
    image, step = pl.pallas_call(
        functools.partial(image_sum_kernel, loads, hots),
        in_specs=[vmem, vmem],
        out_specs=[vmem, vmem],
        out_shape=[
            jax.ShapeDtypeStruct(terms.shape, jnp.float32),
            jax.ShapeDtypeStruct(tile, jnp.float32),
        ],
        scratch_shapes=[
            pltpu.VMEM((loads - 1, rows // loads, cols), jnp.float32),
            pltpu.VMEM((loads,) + tile, jnp.float32),
            pltpu.VMEM((hots,) + tile, jnp.float32),
            pltpu.SemaphoreType.DMA((4, loads - 1)),
            pltpu.SemaphoreType.DMA((2, loads - 1)),
            pltpu.SemaphoreType.DMA((2, hots - 1)),
        ],
        compiler_params=pltpu.CompilerParams(
            collective_id=1, has_side_effects=True, vmem_limit_bytes=40 * MIB
        ),
        name="image_sum",
    )(terms, jnp.broadcast_to(norm, tile))
    return image, step[0, 0]


def hot_sum_kernel(count, in_ref, out_ref, pair, held, parts, pair_sems, part_sems, gather_sems, swap_sems):
    me = lax.axis_index("hot")
    core, chip, chips = lax.rem(me, 2), me // 2, count // 2
    chunk = in_ref.shape[0] // count
    partner = {"hot": me + 1 - 2 * core}
    order = [lax.rem(chip + step, chips) for step in range(1, chips + 1)]
    peers = [{"hot": order[i] * 2 + core} for i in range(chips - 1)]

    def rows(of_core, of_chip):
        return pl.ds(pl.multiple_of((of_core * chips + of_chip) * chunk, 8), chunk)

    greet([partner] + peers)
    halves = []
    for i, at in enumerate(order):
        source = in_ref.at[rows(1 - core, at)]
        halves.append(send(source, pair.at[i], pair_sems.at[0, i], pair_sems.at[1, i], partner))
    copies = []
    for i, at in enumerate(order):
        halves[i].wait()
        held[i] = in_ref[rows(core, at), :] + pair[i]
        if i < chips - 1:
            copies.append(
                send(held.at[i], parts.at[i], part_sems.at[0, i], part_sems.at[1, i], peers[i])
            )
    total = held[chips - 1]
    for i, copy in enumerate(copies):
        copy.wait()
        total += parts[i]
    out_ref[rows(core, chip), :] = total

    mine = out_ref.at[rows(core, chip)]
    copies = [
        send(mine, mine, gather_sems.at[0, i], gather_sems.at[1, i], peers[i])
        for i in range(chips - 1)
    ]
    swaps = [send(mine, mine, swap_sems.at[0, 0], swap_sems.at[1, 0], partner)]
    for i, copy in enumerate(copies):
        copy.wait()
        came = out_ref.at[rows(core, lax.rem(chip + chips - 1 - i, chips))]
        swaps.append(send(came, came, swap_sems.at[0, i + 1], swap_sems.at[1, i + 1], partner))
    for copy in swaps:
        copy.wait()


def hot_sum(terms, count):
    rows, cols = terms.shape
    chunk, chips = rows // count, count // 2
    return pl.pallas_call(
        functools.partial(hot_sum_kernel, count),
        in_specs=[pl.BlockSpec(memory_space=pltpu.VMEM)],
        out_specs=pl.BlockSpec(memory_space=pltpu.VMEM),
        out_shape=jax.ShapeDtypeStruct(terms.shape, terms.dtype),
        scratch_shapes=[
            pltpu.VMEM((chips, chunk, cols), jnp.float32),
            pltpu.VMEM((chips, chunk, cols), jnp.float32),
            pltpu.VMEM((chips - 1, chunk, cols), jnp.float32),
            pltpu.SemaphoreType.DMA((2, chips)),
            pltpu.SemaphoreType.DMA((2, chips - 1)),
            pltpu.SemaphoreType.DMA((2, chips - 1)),
            pltpu.SemaphoreType.DMA((2, chips)),
        ],
        compiler_params=pltpu.CompilerParams(
            collective_id=2, has_side_effects=True, vmem_limit_bytes=40 * MIB
        ),
        name="hot_sum",
    )(terms)


def body(loads, hots, response, forces, measured):
    tiles = tap_major(response)
    strains = load_sum(strain_product(tiles, forces.T), loads)
    residual = measured.T - strains
    padded = hot_sum(load_product(tiles, residual.astype(jnp.bfloat16), hots), hots)
    gradient = padded[:COLS]
    norm = jnp.sum(gradient * gradient)
    terms = strain_product(tiles, gradient.astype(jnp.bfloat16))
    image, step_size = image_sum(terms, norm, loads, hots)
    updated_forces = forces.astype(jnp.float32) + step_size * gradient.T
    return updated_forces, (residual - step_size * image).T


def solution(mesh):
    placed = (P("hot", "load", None), P("load", None), P("hot", None))
    return jax.shard_map(
        functools.partial(body, mesh.shape["load"], mesh.shape["hot"]),
        mesh=mesh,
        in_specs=placed,
        out_specs=(P("load", None), P("hot", None)),
        check_vma=False,
    )
```

```python
import functools

import jax
import jax.numpy as jnp
from jax import lax
from jax.experimental import pallas as pl
from jax.experimental.pallas import tpu as pltpu
from jax.sharding import PartitionSpec as P

TAPS = 128
SEG = 48
CASES = 8
HIST = 128
STEPS = 176
COLS = STEPS * CASES
SEG_COLS = SEG * CASES
MIB = 1 << 20

GROUP = 4
STREAMS = 4
STEP_TAPS = GROUP * STREAMS
WINDOW = -(-(SEG_COLS + (GROUP - 1) * CASES) // 16) * 16


def tap_major_kernel(hots, *refs):
    in_refs, out_refs, held = refs[:STREAMS], refs[STREAMS:-1], refs[-1]
    lanes = held.shape[2]
    each = hots // STREAMS
    for part in range(held.shape[0]):
        loads = slice(part * lanes, (part + 1) * lanes)
        for h in range(hots):
            turned = in_refs[h // each][h % each, loads, :].T
            held[part, pl.ds(h, TAPS, stride=hots), :] = turned.astype(jnp.float32)
        turned = held[part].astype(jnp.bfloat16)
        turned = turned.reshape(TAPS // STEP_TAPS, STREAMS, GROUP, hots, lanes)
        for i, out_ref in enumerate(out_refs):
            out_ref[:, :, loads] = turned[:, i].reshape(TAPS // STREAMS, hots, lanes)


def tap_major(response):
    hots, loads, taps = response.shape
    block = 16
    each = block // STREAMS
    return pl.pallas_call(
        functools.partial(tap_major_kernel, block),
        grid=(hots // block,),
        in_specs=[
            pl.BlockSpec((each, loads, taps), lambda i, part=part: (i * STREAMS + part, 0, 0))
            for part in range(STREAMS)
        ],
        out_specs=[pl.BlockSpec((taps // STREAMS, block, loads), lambda i: (0, i, 0))] * STREAMS,
        out_shape=[
            jax.ShapeDtypeStruct((taps // STREAMS, hots, loads), response.dtype)
        ] * STREAMS,
        scratch_shapes=[pltpu.VMEM((loads // 128, taps * block, 128), jnp.float32)],
        compiler_params=pltpu.CompilerParams(vmem_limit_bytes=40 * MIB),
        cost_estimate=pl.CostEstimate(
            flops=0, bytes_accessed=4 * response.size, transcendentals=0
        ),
        name="tap_major",
    )(*[response] * STREAMS)


def tile_specs(hots, loads):
    return [
        pl.BlockSpec((GROUP, hots, loads), lambda i: (i, 0, 0))
        for _ in range(STREAMS)
    ]


def strain_kernel(even_ref, odd_ref, *refs):
    *tile_refs, out_ref = refs
    step = pl.program_id(0)

    @pl.when(step == 0)
    def _():
        out_ref[...] = jnp.zeros_like(out_ref)

    total = out_ref[...]
    for i in range(STEP_TAPS):
        parity = (HIST - i) % 2
        signal_ref = odd_ref if parity else even_ref
        first = (HIST - i - parity) * CASES - step * (STEP_TAPS * CASES)
        rows = pl.ds(pl.multiple_of(first, 16), SEG_COLS)
        total += lax.dot_general(
            signal_ref[rows, :],
            tile_refs[i // GROUP][i % GROUP],
            (((1,), (1,)), ((), ())),
            preferred_element_type=jnp.float32,
        )
    out_ref[...] = total


def strain_product(tiles, signal):
    _, hots, loads = tiles[0].shape
    odd = jnp.concatenate([signal[CASES:], signal[:CASES]])
    whole = pl.BlockSpec((COLS, loads), lambda i: (0, 0))
    return pl.pallas_call(
        strain_kernel,
        grid=(TAPS // STEP_TAPS,),
        in_specs=[whole, whole, *tile_specs(hots, loads)],
        out_specs=pl.BlockSpec((SEG_COLS, hots), lambda i: (0, 0)),
        out_shape=jax.ShapeDtypeStruct((SEG_COLS, hots), jnp.float32),
        compiler_params=pltpu.CompilerParams(vmem_limit_bytes=40 * MIB),
        cost_estimate=pl.CostEstimate(
            flops=2 * SEG_COLS * TAPS * hots * loads, bytes_accessed=2 * TAPS * hots * loads, transcendentals=0
        ),
        name="strain_product",
    )(signal, odd, *tiles)


def gradient_kernel(hots, strains_ref, *refs):
    *tile_refs, out_ref, held = refs
    step = pl.program_id(0)

    @pl.when(step == 0)
    def _():
        held[...] = jnp.zeros_like(held)

    for i in range(0, STEP_TAPS, GROUP):
        first = (HIST - i - (GROUP - 1)) * CASES - step * (STEP_TAPS * CASES)
        rows = pl.ds(pl.multiple_of(first, CASES), WINDOW)
        tile_ref = tile_refs[i // GROUP]
        tile = tile_ref[...].reshape(GROUP * hots, tile_ref.shape[2])
        held[rows, :] += jnp.dot(strains_ref[...], tile, preferred_element_type=jnp.float32)

    @pl.when(step == TAPS // STEP_TAPS - 1)
    def _():
        out_ref[...] = held[: out_ref.shape[0], :]


def load_product(tiles, strains, parts):
    _, hots, loads = tiles[0].shape
    rows = -(-COLS // (8 * parts)) * 8 * parts
    stacked = jnp.concatenate(
        [
            jnp.pad(
                strains,
                (((GROUP - 1 - i) * CASES, WINDOW - SEG_COLS - (GROUP - 1 - i) * CASES), (0, 0)),
            )
            for i in range(GROUP)
        ],
        axis=1,
    )
    return pl.pallas_call(
        functools.partial(gradient_kernel, hots),
        grid=(TAPS // STEP_TAPS,),
        in_specs=[
            pl.BlockSpec((WINDOW, GROUP * hots), lambda i: (0, 0)),
            *tile_specs(hots, loads),
        ],
        out_specs=pl.BlockSpec((rows, loads), lambda i: (0, 0)),
        out_shape=jax.ShapeDtypeStruct((rows, loads), jnp.float32),
        scratch_shapes=[pltpu.VMEM((max(rows, COLS + 16), loads), jnp.float32)],
        compiler_params=pltpu.CompilerParams(vmem_limit_bytes=40 * MIB),
        cost_estimate=pl.CostEstimate(
            flops=2 * WINDOW * TAPS * hots * loads, bytes_accessed=2 * TAPS * hots * loads, transcendentals=0
        ),
        name="load_product",
    )(stacked, *tiles)


def greet(peers):
    barrier = pltpu.get_barrier_semaphore()
    for peer in peers:
        pl.semaphore_signal(
            barrier, inc=1, device_id=peer, device_id_type=pl.DeviceIdType.MESH
        )
    pl.semaphore_wait(barrier, len(peers))


def send(source, target, send_sem, recv_sem, peer):
    copy = pltpu.make_async_remote_copy(
        src_ref=source,
        dst_ref=target,
        send_sem=send_sem,
        recv_sem=recv_sem,
        device_id=peer,
        device_id_type=pl.DeviceIdType.MESH,
    )
    copy.start()
    return copy


def other(axis, count, step):
    return {axis: lax.rem(lax.axis_index(axis) + step, count)}


def add_over_load(count, in_ref, out_ref, parts, sems):
    me = lax.axis_index("load")
    chunk = in_ref.shape[0] // count

    def rows(index):
        return pl.ds(pl.multiple_of(index * chunk, 8), chunk)

    copies = []
    for step in range(1, count):
        peer = other("load", count, step)
        copies.append(
            send(
                in_ref.at[rows(peer["load"])],
                parts.at[step - 1],
                sems.at[0, step - 1],
                sems.at[1, step - 1],
                peer,
            )
        )
    total = in_ref[rows(me), :]
    for step, copy in enumerate(copies):
        copy.wait()
        total += parts[step]
    out_ref[rows(me), :] = total
    copies = []
    for step in range(1, count):
        mine = out_ref.at[rows(me)]
        peer = other("load", count, step)
        copies.append(send(mine, mine, sems.at[2, step - 1], sems.at[3, step - 1], peer))
    for copy in copies:
        copy.wait()


def load_sum_kernel(count, in_ref, out_ref, parts, sems):
    greet([other("load", count, step) for step in range(1, count)])
    add_over_load(count, in_ref, out_ref, parts, sems)


def load_sum(terms, count):
    rows, cols = terms.shape
    return pl.pallas_call(
        functools.partial(load_sum_kernel, count),
        in_specs=[pl.BlockSpec(memory_space=pltpu.VMEM)],
        out_specs=pl.BlockSpec(memory_space=pltpu.VMEM),
        out_shape=jax.ShapeDtypeStruct(terms.shape, terms.dtype),
        scratch_shapes=[
            pltpu.VMEM((count - 1, rows // count, cols), jnp.float32),
            pltpu.SemaphoreType.DMA((4, count - 1)),
        ],
        compiler_params=pltpu.CompilerParams(
            collective_id=0, has_side_effects=True, vmem_limit_bytes=40 * MIB
        ),
        name="load_sum",
    )(terms)


def image_sum_kernel(
    loads, hots, in_ref, norm_ref, out_ref, step_ref, parts, load_norms, hot_norms, sems, load_sems, hot_sems
):
    load, hot = lax.axis_index("load"), lax.axis_index("hot")
    load_peers = [other("load", loads, step) for step in range(1, loads)]
    hot_peers = [other("hot", hots, step) for step in range(1, hots)]
    greet(load_peers + hot_peers)

    load_norms[load] = norm_ref[...]
    copies = []
    for i, peer in enumerate(load_peers):
        mine = load_norms.at[load]
        copies.append(send(mine, mine, load_sems.at[0, i], load_sems.at[1, i], peer))
    add_over_load(loads, in_ref, out_ref, parts, sems)
    image = out_ref[...]
    hot_norms[hot] = jnp.full(hot_norms.shape[1:], jnp.sum(image * image))
    for i, peer in enumerate(hot_peers):
        mine = hot_norms.at[hot]
        copies.append(send(mine, mine, hot_sems.at[0, i], hot_sems.at[1, i], peer))
    for copy in copies:
        copy.wait()
    step_ref[...] = jnp.sum(load_norms[...], axis=0) / jnp.sum(hot_norms[...], axis=0)


def image_sum(terms, norm, loads, hots):
    rows, cols = terms.shape
    tile = (8, 128)
    vmem = pl.BlockSpec(memory_space=pltpu.VMEM)
    image, step = pl.pallas_call(
        functools.partial(image_sum_kernel, loads, hots),
        in_specs=[vmem, vmem],
        out_specs=[vmem, vmem],
        out_shape=[
            jax.ShapeDtypeStruct(terms.shape, jnp.float32),
            jax.ShapeDtypeStruct(tile, jnp.float32),
        ],
        scratch_shapes=[
            pltpu.VMEM((loads - 1, rows // loads, cols), jnp.float32),
            pltpu.VMEM((loads,) + tile, jnp.float32),
            pltpu.VMEM((hots,) + tile, jnp.float32),
            pltpu.SemaphoreType.DMA((4, loads - 1)),
            pltpu.SemaphoreType.DMA((2, loads - 1)),
            pltpu.SemaphoreType.DMA((2, hots - 1)),
        ],
        compiler_params=pltpu.CompilerParams(
            collective_id=1, has_side_effects=True, vmem_limit_bytes=40 * MIB
        ),
        name="image_sum",
    )(terms, jnp.broadcast_to(norm, tile))
    return image, step


def hot_sum_kernel(count, in_ref, out_ref, pair, held, parts, pair_sems, part_sems, gather_sems, swap_sems):
    me = lax.axis_index("hot")
    core, chip, chips = lax.rem(me, 2), me // 2, count // 2
    chunk = in_ref.shape[0] // count
    partner = {"hot": me + 1 - 2 * core}
    order = [lax.rem(chip + step, chips) for step in range(1, chips + 1)]
    peers = [{"hot": order[i] * 2 + core} for i in range(chips - 1)]

    def rows(of_core, of_chip):
        return pl.ds(pl.multiple_of((of_core * chips + of_chip) * chunk, 8), chunk)

    greet([partner] + peers)
    halves = []
    for i, at in enumerate(order):
        source = in_ref.at[rows(1 - core, at)]
        halves.append(send(source, pair.at[i], pair_sems.at[0, i], pair_sems.at[1, i], partner))
    copies = []
    for i, at in enumerate(order):
        halves[i].wait()
        held[i] = in_ref[rows(core, at), :] + pair[i]
        if i < chips - 1:
            copies.append(
                send(held.at[i], parts.at[i], part_sems.at[0, i], part_sems.at[1, i], peers[i])
            )
    total = held[chips - 1]
    for i, copy in enumerate(copies):
        copy.wait()
        total += parts[i]
    out_ref[rows(core, chip), :] = total

    mine = out_ref.at[rows(core, chip)]
    copies = [
        send(mine, mine, gather_sems.at[0, i], gather_sems.at[1, i], peers[i])
        for i in range(chips - 1)
    ]
    swaps = [send(mine, mine, swap_sems.at[0, 0], swap_sems.at[1, 0], partner)]
    for i, copy in enumerate(copies):
        copy.wait()
        came = out_ref.at[rows(core, lax.rem(chip + chips - 1 - i, chips))]
        swaps.append(send(came, came, swap_sems.at[0, i + 1], swap_sems.at[1, i + 1], partner))
    for copy in swaps:
        copy.wait()


def hot_sum(terms, count):
    rows, cols = terms.shape
    chunk, chips = rows // count, count // 2
    return pl.pallas_call(
        functools.partial(hot_sum_kernel, count),
        in_specs=[pl.BlockSpec(memory_space=pltpu.VMEM)],
        out_specs=pl.BlockSpec(memory_space=pltpu.VMEM),
        out_shape=jax.ShapeDtypeStruct(terms.shape, terms.dtype),
        scratch_shapes=[
            pltpu.VMEM((chips, chunk, cols), jnp.float32),
            pltpu.VMEM((chips, chunk, cols), jnp.float32),
            pltpu.VMEM((chips - 1, chunk, cols), jnp.float32),
            pltpu.SemaphoreType.DMA((2, chips)),
            pltpu.SemaphoreType.DMA((2, chips - 1)),
            pltpu.SemaphoreType.DMA((2, chips - 1)),
            pltpu.SemaphoreType.DMA((2, chips)),
        ],
        compiler_params=pltpu.CompilerParams(
            collective_id=2, has_side_effects=True, vmem_limit_bytes=40 * MIB
        ),
        name="hot_sum",
    )(terms)


def update_kernel(step_ref, forces_ref, gradient_ref, residual_ref, image_ref, forces_out, residual_out):
    step_size = step_ref[:1, :1]
    forces_out[...] = forces_ref[...].astype(jnp.float32) + step_size * gradient_ref[:COLS, :].T

    @pl.when(pl.program_id(0) == 0)
    def _():
        residual_out[...] = (residual_ref[...] - step_size * image_ref[...]).T


def update(step, forces, gradient, residual, image):
    loads, hots = forces.shape[0], residual.shape[1]
    block = 128

    def whole(array):
        return pl.BlockSpec(array.shape, lambda i: (0, 0))

    by_load = pl.BlockSpec((block, COLS), lambda i: (i, 0))
    return pl.pallas_call(
        update_kernel,
        grid=(loads // block,),
        in_specs=[
            whole(step),
            by_load,
            pl.BlockSpec((gradient.shape[0], block), lambda i: (0, i)),
            whole(residual),
            whole(image),
        ],
        out_specs=[by_load, pl.BlockSpec((hots, SEG_COLS), lambda i: (0, 0))],
        out_shape=[
            jax.ShapeDtypeStruct((loads, COLS), jnp.float32),
            jax.ShapeDtypeStruct((hots, SEG_COLS), jnp.float32),
        ],
        compiler_params=pltpu.CompilerParams(vmem_limit_bytes=40 * MIB),
        name="update",
    )(step, forces, gradient, residual, image)


def body(loads, hots, response, forces, measured):
    tiles = tap_major(response)
    strains = load_sum(strain_product(tiles, forces.T), loads)
    residual = measured.T - strains
    padded = hot_sum(load_product(tiles, residual.astype(jnp.bfloat16), hots), hots)
    gradient = padded[:COLS]
    norm = jnp.sum(gradient * gradient)
    terms = strain_product(tiles, gradient.astype(jnp.bfloat16))
    image, step = image_sum(terms, norm, loads, hots)
    return tuple(update(step, forces, padded, residual, image))


def solution(mesh):
    placed = (P("hot", "load", None), P("load", None), P("hot", None))
    return jax.shard_map(
        functools.partial(body, mesh.shape["load"], mesh.shape["hot"]),
        mesh=mesh,
        in_specs=placed,
        out_specs=(P("load", None), P("hot", None)),
        check_vma=False,
    )
```

```python
import functools

import jax
import jax.numpy as jnp
from jax import lax
from jax.experimental import pallas as pl
from jax.experimental.pallas import tpu as pltpu
from jax.sharding import PartitionSpec as P

TAPS = 128
SEG = 48
CASES = 8
HIST = 128
STEPS = 176
COLS = STEPS * CASES
SEG_COLS = SEG * CASES
MIB = 1 << 20

GROUP = 4
STREAMS = 4
STEP_TAPS = GROUP * STREAMS
WINDOW = -(-(SEG_COLS + (GROUP - 1) * CASES) // 16) * 16


def tap_major_kernel(hots, *refs):
    in_refs, out_refs, held = refs[:STREAMS], refs[STREAMS:-1], refs[-1]
    lanes = held.shape[2]
    each = hots // STREAMS
    for part in range(held.shape[0]):
        loads = slice(part * lanes, (part + 1) * lanes)
        for h in range(hots):
            turned = in_refs[h // each][h % each, loads, :].T
            held[part, pl.ds(h, TAPS, stride=hots), :] = turned.astype(jnp.float32)
        turned = held[part].astype(jnp.bfloat16)
        turned = turned.reshape(TAPS // STEP_TAPS, STREAMS, GROUP, hots, lanes)
        for i, out_ref in enumerate(out_refs):
            out_ref[:, :, loads] = turned[:, i].reshape(TAPS // STREAMS, hots, lanes)


def tap_major(response):
    hots, loads, taps = response.shape
    block = 16
    each = block // STREAMS
    return pl.pallas_call(
        functools.partial(tap_major_kernel, block),
        grid=(hots // block,),
        in_specs=[
            pl.BlockSpec((each, loads, taps), lambda i, part=part: (i * STREAMS + part, 0, 0))
            for part in range(STREAMS)
        ],
        out_specs=[pl.BlockSpec((taps // STREAMS, block, loads), lambda i: (0, i, 0))] * STREAMS,
        out_shape=[
            jax.ShapeDtypeStruct((taps // STREAMS, hots, loads), response.dtype)
        ] * STREAMS,
        scratch_shapes=[pltpu.VMEM((loads // 128, taps * block, 128), jnp.float32)],
        compiler_params=pltpu.CompilerParams(vmem_limit_bytes=56 * MIB),
        cost_estimate=pl.CostEstimate(
            flops=0, bytes_accessed=4 * response.size, transcendentals=0
        ),
        name="tap_major",
    )(*[response] * STREAMS)


def tile_specs(hots, loads):
    return [
        pl.BlockSpec((GROUP, hots, loads), lambda i: (i, 0, 0))
        for _ in range(STREAMS)
    ]


def strain_kernel(even_ref, odd_ref, *refs):
    *tile_refs, out_ref = refs
    step = pl.program_id(0)

    @pl.when(step == 0)
    def _():
        out_ref[...] = jnp.zeros_like(out_ref)

    total = out_ref[...]
    for i in range(STEP_TAPS):
        parity = (HIST - i) % 2
        signal_ref = odd_ref if parity else even_ref
        first = (HIST - i - parity) * CASES - step * (STEP_TAPS * CASES)
        rows = pl.ds(pl.multiple_of(first, 16), SEG_COLS)
        total += lax.dot_general(
            signal_ref[rows, :],
            tile_refs[i // GROUP][i % GROUP],
            (((1,), (1,)), ((), ())),
            preferred_element_type=jnp.float32,
        )
    out_ref[...] = total


def strain_product(tiles, signal):
    _, hots, loads = tiles[0].shape
    odd = jnp.concatenate([signal[CASES:], signal[:CASES]])
    whole = pl.BlockSpec((COLS, loads), lambda i: (0, 0))
    return pl.pallas_call(
        strain_kernel,
        grid=(TAPS // STEP_TAPS,),
        in_specs=[whole, whole, *tile_specs(hots, loads)],
        out_specs=pl.BlockSpec((SEG_COLS, hots), lambda i: (0, 0)),
        out_shape=jax.ShapeDtypeStruct((SEG_COLS, hots), jnp.float32),
        compiler_params=pltpu.CompilerParams(vmem_limit_bytes=56 * MIB),
        cost_estimate=pl.CostEstimate(
            flops=2 * SEG_COLS * TAPS * hots * loads, bytes_accessed=2 * TAPS * hots * loads, transcendentals=0
        ),
        name="strain_product",
    )(signal, odd, *tiles)


def gradient_kernel(hots, strains_ref, *refs):
    *tile_refs, out_ref, held = refs
    step = pl.program_id(0)

    @pl.when(step == 0)
    def _():
        held[...] = jnp.zeros_like(held)

    for i in range(0, STEP_TAPS, GROUP):
        first = (HIST - i - (GROUP - 1)) * CASES - step * (STEP_TAPS * CASES)
        rows = pl.ds(pl.multiple_of(first, CASES), WINDOW)
        tile_ref = tile_refs[i // GROUP]
        tile = tile_ref[...].reshape(GROUP * hots, tile_ref.shape[2])
        held[rows, :] += jnp.dot(strains_ref[...], tile, preferred_element_type=jnp.float32)

    @pl.when(step == TAPS // STEP_TAPS - 1)
    def _():
        out_ref[...] = held[: out_ref.shape[0], :]


def load_product(tiles, strains, parts):
    _, hots, loads = tiles[0].shape
    rows = -(-COLS // (8 * parts)) * 8 * parts
    stacked = jnp.concatenate(
        [
            jnp.pad(
                strains,
                (((GROUP - 1 - i) * CASES, WINDOW - SEG_COLS - (GROUP - 1 - i) * CASES), (0, 0)),
            )
            for i in range(GROUP)
        ],
        axis=1,
    )
    return pl.pallas_call(
        functools.partial(gradient_kernel, hots),
        grid=(TAPS // STEP_TAPS,),
        in_specs=[
            pl.BlockSpec((WINDOW, GROUP * hots), lambda i: (0, 0)),
            *tile_specs(hots, loads),
        ],
        out_specs=pl.BlockSpec((rows, loads), lambda i: (0, 0)),
        out_shape=jax.ShapeDtypeStruct((rows, loads), jnp.float32),
        scratch_shapes=[pltpu.VMEM((max(rows, COLS + 16), loads), jnp.float32)],
        compiler_params=pltpu.CompilerParams(vmem_limit_bytes=56 * MIB),
        cost_estimate=pl.CostEstimate(
            flops=2 * WINDOW * TAPS * hots * loads, bytes_accessed=2 * TAPS * hots * loads, transcendentals=0
        ),
        name="load_product",
    )(stacked, *tiles)


def greet(peers):
    barrier = pltpu.get_barrier_semaphore()
    for peer in peers:
        pl.semaphore_signal(
            barrier, inc=1, device_id=peer, device_id_type=pl.DeviceIdType.MESH
        )
    pl.semaphore_wait(barrier, len(peers))


def send(source, target, send_sem, recv_sem, peer):
    copy = pltpu.make_async_remote_copy(
        src_ref=source,
        dst_ref=target,
        send_sem=send_sem,
        recv_sem=recv_sem,
        device_id=peer,
        device_id_type=pl.DeviceIdType.MESH,
    )
    copy.start()
    return copy


def other(axis, count, step):
    return {axis: lax.rem(lax.axis_index(axis) + step, count)}


def add_over_load(count, in_ref, out_ref, parts, sems):
    me = lax.axis_index("load")
    chunk = in_ref.shape[0] // count

    def rows(index):
        return pl.ds(pl.multiple_of(index * chunk, 8), chunk)

    copies = []
    for step in range(1, count):
        peer = other("load", count, step)
        copies.append(
            send(
                in_ref.at[rows(peer["load"])],
                parts.at[step - 1],
                sems.at[0, step - 1],
                sems.at[1, step - 1],
                peer,
            )
        )
    total = in_ref[rows(me), :]
    for step, copy in enumerate(copies):
        copy.wait()
        total += parts[step]
    out_ref[rows(me), :] = total
    copies = []
    for step in range(1, count):
        mine = out_ref.at[rows(me)]
        peer = other("load", count, step)
        copies.append(send(mine, mine, sems.at[2, step - 1], sems.at[3, step - 1], peer))
    for copy in copies:
        copy.wait()


def load_sum_kernel(count, in_ref, out_ref, parts, sems):
    greet([other("load", count, step) for step in range(1, count)])
    add_over_load(count, in_ref, out_ref, parts, sems)


def load_sum(terms, count):
    rows, cols = terms.shape
    return pl.pallas_call(
        functools.partial(load_sum_kernel, count),
        in_specs=[pl.BlockSpec(memory_space=pltpu.VMEM)],
        out_specs=pl.BlockSpec(memory_space=pltpu.VMEM),
        out_shape=jax.ShapeDtypeStruct(terms.shape, terms.dtype),
        scratch_shapes=[
            pltpu.VMEM((count - 1, rows // count, cols), jnp.float32),
            pltpu.SemaphoreType.DMA((4, count - 1)),
        ],
        compiler_params=pltpu.CompilerParams(
            collective_id=0, has_side_effects=True, vmem_limit_bytes=56 * MIB
        ),
        name="load_sum",
    )(terms)


def image_sum_kernel(
    loads, hots, in_ref, norm_ref, out_ref, step_ref, parts, load_norms, hot_norms, sems, load_sems, hot_sems
):
    load, hot = lax.axis_index("load"), lax.axis_index("hot")
    load_peers = [other("load", loads, step) for step in range(1, loads)]
    hot_peers = [other("hot", hots, step) for step in range(1, hots)]
    greet(load_peers + hot_peers)

    load_norms[load] = norm_ref[...]
    copies = []
    for i, peer in enumerate(load_peers):
        mine = load_norms.at[load]
        copies.append(send(mine, mine, load_sems.at[0, i], load_sems.at[1, i], peer))
    add_over_load(loads, in_ref, out_ref, parts, sems)
    image = out_ref[...]
    hot_norms[hot] = jnp.full(hot_norms.shape[1:], jnp.sum(image * image))
    for i, peer in enumerate(hot_peers):
        mine = hot_norms.at[hot]
        copies.append(send(mine, mine, hot_sems.at[0, i], hot_sems.at[1, i], peer))
    for copy in copies:
        copy.wait()
    step_ref[...] = jnp.sum(load_norms[...], axis=0) / jnp.sum(hot_norms[...], axis=0)


def image_sum(terms, norm, loads, hots):
    rows, cols = terms.shape
    tile = (8, 128)
    vmem = pl.BlockSpec(memory_space=pltpu.VMEM)
    image, step = pl.pallas_call(
        functools.partial(image_sum_kernel, loads, hots),
        in_specs=[vmem, vmem],
        out_specs=[vmem, vmem],
        out_shape=[
            jax.ShapeDtypeStruct(terms.shape, jnp.float32),
            jax.ShapeDtypeStruct(tile, jnp.float32),
        ],
        scratch_shapes=[
            pltpu.VMEM((loads - 1, rows // loads, cols), jnp.float32),
            pltpu.VMEM((loads,) + tile, jnp.float32),
            pltpu.VMEM((hots,) + tile, jnp.float32),
            pltpu.SemaphoreType.DMA((4, loads - 1)),
            pltpu.SemaphoreType.DMA((2, loads - 1)),
            pltpu.SemaphoreType.DMA((2, hots - 1)),
        ],
        compiler_params=pltpu.CompilerParams(
            collective_id=1, has_side_effects=True, vmem_limit_bytes=56 * MIB
        ),
        name="image_sum",
    )(terms, jnp.broadcast_to(norm, tile))
    return image, step


def hot_sum_kernel(count, in_ref, out_ref, pair, held, parts, pair_sems, part_sems, gather_sems, swap_sems):
    me = lax.axis_index("hot")
    core, chip, chips = lax.rem(me, 2), me // 2, count // 2
    chunk = in_ref.shape[0] // count
    partner = {"hot": me + 1 - 2 * core}
    order = [lax.rem(chip + step, chips) for step in range(1, chips + 1)]
    peers = [{"hot": order[i] * 2 + core} for i in range(chips - 1)]

    def rows(of_core, of_chip):
        return pl.ds(pl.multiple_of((of_core * chips + of_chip) * chunk, 8), chunk)

    greet([partner] + peers)
    halves = []
    for i, at in enumerate(order):
        source = in_ref.at[rows(1 - core, at)]
        halves.append(send(source, pair.at[i], pair_sems.at[0, i], pair_sems.at[1, i], partner))
    copies = []
    for i, at in enumerate(order):
        halves[i].wait()
        held[i] = in_ref[rows(core, at), :] + pair[i]
        if i < chips - 1:
            copies.append(
                send(held.at[i], parts.at[i], part_sems.at[0, i], part_sems.at[1, i], peers[i])
            )
    total = held[chips - 1]
    for i, copy in enumerate(copies):
        copy.wait()
        total += parts[i]
    out_ref[rows(core, chip), :] = total

    mine = out_ref.at[rows(core, chip)]
    copies = [
        send(mine, mine, gather_sems.at[0, i], gather_sems.at[1, i], peers[i])
        for i in range(chips - 1)
    ]
    swaps = [send(mine, mine, swap_sems.at[0, 0], swap_sems.at[1, 0], partner)]
    for i, copy in enumerate(copies):
        copy.wait()
        came = out_ref.at[rows(core, lax.rem(chip + chips - 1 - i, chips))]
        swaps.append(send(came, came, swap_sems.at[0, i + 1], swap_sems.at[1, i + 1], partner))
    for copy in swaps:
        copy.wait()


def hot_sum(terms, count):
    rows, cols = terms.shape
    chunk, chips = rows // count, count // 2
    return pl.pallas_call(
        functools.partial(hot_sum_kernel, count),
        in_specs=[pl.BlockSpec(memory_space=pltpu.VMEM)],
        out_specs=pl.BlockSpec(memory_space=pltpu.VMEM),
        out_shape=jax.ShapeDtypeStruct(terms.shape, terms.dtype),
        scratch_shapes=[
            pltpu.VMEM((chips, chunk, cols), jnp.float32),
            pltpu.VMEM((chips, chunk, cols), jnp.float32),
            pltpu.VMEM((chips - 1, chunk, cols), jnp.float32),
            pltpu.SemaphoreType.DMA((2, chips)),
            pltpu.SemaphoreType.DMA((2, chips - 1)),
            pltpu.SemaphoreType.DMA((2, chips - 1)),
            pltpu.SemaphoreType.DMA((2, chips)),
        ],
        compiler_params=pltpu.CompilerParams(
            collective_id=2, has_side_effects=True, vmem_limit_bytes=56 * MIB
        ),
        name="hot_sum",
    )(terms)


def update_kernel(step_ref, forces_ref, gradient_ref, residual_ref, image_ref, forces_out, residual_out):
    step_size = step_ref[:1, :1]
    forces_out[...] = forces_ref[...].astype(jnp.float32) + step_size * gradient_ref[:COLS, :].T

    @pl.when(pl.program_id(0) == 0)
    def _():
        residual_out[...] = (residual_ref[...] - step_size * image_ref[...]).T


def update(step, forces, gradient, residual, image):
    loads, hots = forces.shape[0], residual.shape[1]
    block = 128

    def whole(array):
        return pl.BlockSpec(array.shape, lambda i: (0, 0))

    by_load = pl.BlockSpec((block, COLS), lambda i: (i, 0))
    return pl.pallas_call(
        update_kernel,
        grid=(loads // block,),
        in_specs=[
            whole(step),
            by_load,
            pl.BlockSpec((gradient.shape[0], block), lambda i: (0, i)),
            whole(residual),
            whole(image),
        ],
        out_specs=[by_load, pl.BlockSpec((hots, SEG_COLS), lambda i: (0, 0))],
        out_shape=[
            jax.ShapeDtypeStruct((loads, COLS), jnp.float32),
            jax.ShapeDtypeStruct((hots, SEG_COLS), jnp.float32),
        ],
        compiler_params=pltpu.CompilerParams(vmem_limit_bytes=56 * MIB),
        name="update",
    )(step, forces, gradient, residual, image)


def body(loads, hots, response, forces, measured):
    tiles = tap_major(response)
    strains = load_sum(strain_product(tiles, forces.T), loads)
    residual = measured.T - strains
    padded = hot_sum(load_product(tiles, residual.astype(jnp.bfloat16), hots), hots)
    gradient = padded[:COLS]
    norm = jnp.sum(gradient * gradient)
    terms = strain_product(tiles, gradient.astype(jnp.bfloat16))
    image, step = image_sum(terms, norm, loads, hots)
    return tuple(update(step, forces, padded, residual, image))


def solution(mesh):
    placed = (P("hot", "load", None), P("load", None), P("hot", None))
    return jax.shard_map(
        functools.partial(body, mesh.shape["load"], mesh.shape["hot"]),
        mesh=mesh,
        in_specs=placed,
        out_specs=(P("load", None), P("hot", None)),
        check_vma=False,
    )
```
